256 devices in a mesh: grp: 2 (over core), ctx: 32 (over y, z), hd: 4 (over x).
Axes of the slice: x: 4, y: 4, z: 8, core: 2. Of those that a mesh axis runs over, the one named last changes fastest.
Arguments:
- q_nope: bfloat16 [2, 8192, 8192], P('grp', ('ctx', 'hd')), may hold values from -6 to 6
- q_rope: bfloat16 [2, 8192, 4096], P('grp', ('ctx', 'hd')), may hold values from -256 to 256
- prompt_latent: bfloat16 [2, 8192, 512], P('grp', ('ctx', 'hd')), may hold values from -6 to 6
- prompt_rope: bfloat16 [2, 4096, 128], P('grp', ('ctx', 'hd')), may hold values from -4 to 4
- prompt_lists: int32 [2, 128, 16], P('grp'), may hold values from 0 to 127, as said below
- owner_map: int32 [2, 128, 1], P('grp'), may hold values from 0 to 31; in each aligned block of 128 rows (0 to 127, 128 to 255, ..., all dimensions but the last counted through in order) at most 8 rows name the same one
- w_uk: bfloat16 [64, 128, 512], P('hd'), may hold values from -0.5 to 0.5
- w_uv: bfloat16 [64, 512, 128], P('hd'), may hold values from -0.75 to 0.75
- dec_nope: bfloat16 [2, 64, 8192], P('grp', None, 'hd'), may hold values from -6 to 6
- dec_rope: bfloat16 [2, 64, 4096], P('grp', None, 'hd'), may hold values from -256 to 256
- store_latent: bfloat16 [2, 4, 128, 64, 512], P('grp', None, 'ctx'), may hold values from -6 to 6
- store_rope: bfloat16 [2, 4, 128, 4096], P('grp', None, 'ctx'), may hold values from -4 to 4
- lengths: int32 [2, 4], P('grp'), may hold values from 961 to 8192, as said below
- page_lists: int32 [2, 4, 16], P('grp'), may hold values from 0 to 127, as said below
Outputs:
- pre_out: bfloat16 [2, 8192, 8192], P('grp', 'ctx', 'hd')
- dec_out: bfloat16 [2, 64, 8192], P('grp', 'ctx', 'hd')
- landed_latent: bfloat16 [2, 256, 64, 512], P('grp', 'ctx')
- landed_rope: bfloat16 [2, 256, 4096], P('grp', 'ctx')
The draws below stay inside these ranges and needn't reach their ends.
Inputs may be any that keep to these rules, and one draw needn't show every extreme that they name: `prompt_lists`: row b of a group lists 16 distinct blocks: b itself, min(b, 15) blocks before b, and later blocks for the rest. `owner_map`: each owner receives at most 8 of the pages of one group's prompt. `lengths`: some request of each group holds all 128 pages full. `page_lists`: each request lists 16 distinct pages that hold cached tokens, always including its last two such pages.
All inputs are finite; a program needn't handle non-finite values.
Results may differ from the reference program's by a relative error of at most 0.0075.
Values may be sent and summed in bfloat16 or wider, within the bound.
No kernel may reach another device: no remote copies, remote signals or barrier semaphores. Data moves between devices by JAX's collectives and lax.ppermute only.
A program may use at most 128 MiB of HBM per device.

```python
import math
import jax
import jax.numpy as jnp
import numpy as np
from jax import lax

H = 64
NOPE = 128
ROPE = 64
LAT = 512
VDIM = 128
BLK = 64
TOPK = 16
ROWS_REQ = 16
DREQ = 4
PPR_DEV = 4
TPRE = 8192
NBLK = 128
NEW_CAP = 8
DROWS = 64
PPR = 128
N_CTX = 32


def prompt_base(key):
    k_rotary, k_query = jax.random.split(key, 2)
    rotary = jnp.clip(jax.random.normal(k_rotary, (2, TPRE, ROPE), jnp.float32), -4.0, 4.0)
    queries = jnp.clip(jax.random.normal(k_query, (2, TPRE, H, ROPE), jnp.float32), -4.0, 4.0)
    return (rotary, queries)


def decode_base(key):
    k_len = jax.random.fold_in(key, 0)
    k_full = jax.random.fold_in(key, 1)
    k_short = jax.random.fold_in(key, 2)
    k_rotary = jax.random.fold_in(key, 3)
    k_query = jax.random.fold_in(key, 4)
    k_low = jax.random.fold_in(key, 7)
    lowest = (TOPK - 1) * BLK + 1
    drawn = jax.random.randint(k_len, (2, DREQ), lowest, PPR * BLK + 1)
    low_drawn = jax.random.randint(k_low, (2, DREQ), lowest, TOPK * BLK + 1)
    full_index = jax.random.randint(k_full, (2, 1), 0, DREQ)
    short_index = (full_index + jax.random.randint(k_short, (2, 1), 1, DREQ)) % DREQ
    requests = jnp.arange(DREQ)[None, :]
    lengths_drawn = jnp.where(requests == full_index, PPR * BLK, jnp.where(requests == short_index, low_drawn, drawn))
    rotary = jnp.clip(jax.random.normal(k_rotary, (2, DREQ, PPR * BLK, ROPE), jnp.float32), -4.0, 4.0)
    queries = jnp.clip(jax.random.normal(k_query, (2, DROWS, H, ROPE), jnp.float32), -4.0, 4.0)
    return (lengths_drawn, rotary, queries)


def draw_q_rope(key, part):
    rotary, queries = prompt_base(key)
    return queries.reshape(2, TPRE, H * ROPE).astype(jnp.bfloat16)


def draw_prompt_rope(key, part):
    rotary, queries = prompt_base(key)
    return rotary.reshape(2, TPRE // 2, 2 * ROPE).astype(jnp.bfloat16)


def draw_prompt_lists(key, part):
    key = jax.random.fold_in(key, 31)
    blocks = jnp.arange(NBLK, dtype=jnp.int32)
    tiers = jnp.where(blocks[None, :] == blocks[:, None], 3, jnp.where(blocks[None, :] < blocks[:, None], 2, 1))
    jitter = jax.random.randint(key, (2, NBLK, NBLK), 0, 1024)
    ranking = tiers[None, :, :] * 4194304 + jitter * NBLK + blocks[None, None, :]
    return lax.top_k(ranking, TOPK)[1].astype(jnp.int32)


def draw_dec_rope(key, part):
    lengths_drawn, rotary, queries = decode_base(key)
    return queries.reshape(2, DROWS, H * ROPE).astype(jnp.bfloat16)


def draw_store_rope(key, part):
    lengths_drawn, rotary, queries = decode_base(key)
    return rotary.reshape(2, DREQ, PPR, BLK * ROPE).astype(jnp.bfloat16)


def draw_lengths(key, part):
    lengths_drawn, rotary, queries = decode_base(key)
    return lengths_drawn.astype(jnp.int32)


def draw_page_lists(key, part):
    lengths_drawn, rotary, queries = decode_base(key)
    key = jax.random.fold_in(key, 24)
    k_hot_first, k_hot_second, k_jitter = jax.random.split(key, 3)
    valid_pages = ((lengths_drawn + BLK - 1) // BLK)[:, :, None]
    page_index = jnp.arange(PPR, dtype=jnp.int32)
    shard_index = page_index // PPR_DEV
    hot_first = jax.random.randint(k_hot_first, (2, DREQ, 1), 0, N_CTX)
    hot_second = jax.random.randint(k_hot_second, (2, DREQ, 1), 0, N_CTX)
    hot_pages = (shard_index[None, None, :] == hot_first) | (shard_index[None, None, :] == hot_second)
    recent = (page_index[None, None, :] >= valid_pages - 2) & (page_index[None, None, :] < valid_pages)
    earlier = page_index[None, None, :] < valid_pages - 2
    tiers = jnp.where(recent, 3, jnp.where(earlier, 1 + hot_pages.astype(jnp.int32), 0))
    jitter = jax.random.randint(k_jitter, (2, DREQ, PPR), 0, 1024)
    ranking = tiers * 4194304 + jitter * PPR + page_index[None, None, :]
    return lax.top_k(ranking, TOPK)[1].astype(jnp.int32)


def shard_levels(key, extent, cuts, low, largest):
    factor_of, own = 1.0, jax.random.fold_in(key, 6)
    for dim, parts in cuts:
        draws = jnp.exp(jax.random.uniform(jax.random.fold_in(own, dim), (parts,), jnp.float32, low / len(cuts), largest / len(cuts)))
        factor_of = factor_of * jnp.repeat(draws, extent[dim] // parts).reshape([-1 if axis == dim else 1 for axis in range(len(extent))])
    return factor_of


def assign_block(key, own, number, rows, amount, top, most, slope):
    order = jax.random.permutation(key, amount)
    crowded, ordinary = shares(amount, rows * top, most, slope, True), shares(amount, rows * top, most, slope, False)
    places = jnp.arange(amount)

    def named(sizes, rotation):
        used = int((sizes > 0).sum())
        fixed = max(1, used // 4)
        moved = fixed + (places - fixed + rotation * (used - fixed)) % max(1, amount - fixed)
        return jnp.zeros((amount,), jnp.int32).at[order[jnp.where(places < fixed, places, moved)]].set(jnp.asarray(sizes, jnp.int32))

    sizes = jnp.where(number % 4 == 0, named(crowded, number // 4), named(ordinary, number - number // 4 - 1))
    mixed = jax.random.permutation(jax.random.fold_in(own, 3), amount)
    source_of, taker = mixed[0:amount // 2 * 2:2], mixed[1:amount // 2 * 2:2]
    slack = jnp.minimum(sizes[source_of] - 1, most - sizes[taker]) // 2
    slack = jnp.where((source_of == order[0]) | (taker == order[0]) | (sizes[taker] == 0), 0, jnp.maximum(slack, 0))
    moved = jax.random.randint(jax.random.fold_in(own, 4), (amount // 2,), 0, 1 << 20) % (slack + 1)
    sizes = sizes.at[source_of].add(-moved).at[taker].add(moved)
    members = jnp.searchsorted(jnp.cumsum(sizes), jnp.arange(rows * top), side="right").astype(jnp.int32)
    listing = members.reshape(top, rows).T
    listing = listing[jax.random.permutation(jax.random.fold_in(own, 1), rows)]
    rotation = jax.random.randint(jax.random.fold_in(own, 2), (rows, 1), 0, top)
    return jnp.take_along_axis(listing, (jnp.arange(top)[None, :] + rotation) % top, axis=1)


def shares(number_of, total, limit, skew, full):
    weights = [(1 << 20) // math.isqrt(rank ** skew) + 1 for rank in range(1, number_of + 1)]
    largest = limit if full else min(limit, max(-(-total // number_of), total * weights[0] // sum(weights)))
    least = 1 if total - largest >= number_of - 1 else 0
    counts, surplus = [largest] + [least] * (number_of - 1), total - largest - least * (number_of - 1)
    while surplus > 0:
        free = [i for i in range(1, number_of) if counts[i] < largest] or [i for i in range(1, number_of) if counts[i] < limit]
        pool, left = sum([weights[i] for i in free]), surplus
        for i in free:
            more = min(limit - counts[i], max(1, left * weights[i] // pool), surplus)
            counts[i] = counts[i] + more
            surplus = surplus - more
    return np.array(counts)


def centred(stream_key, extent, deviation, reach, shards=(), kind=jnp.bfloat16):
    entries = jax.random.normal(stream_key, extent, jnp.float32) * deviation
    if len(shards) > 0:
        entries = shard_levels(stream_key, extent, shards, -0.22, 0.18) * entries
    return jnp.clip(entries, min=-reach, max=reach).astype(kind)


def setup_inputs(seed: int = 0) -> dict:
    seeds = jax.random.split(jax.random.key(seed), 15)
    q_nope = centred(seeds[0], (2, TPRE, H * NOPE), 1.0, 6.0, ((0, 2), (1, 128)))
    q_rope = draw_q_rope(jax.random.fold_in(seeds[14], 71), 0)
    prompt_latent = centred(seeds[2], (2, TPRE, LAT), 1.0, 6.0, ((0, 2), (1, 128)))
    prompt_rope = draw_prompt_rope(jax.random.fold_in(seeds[14], 71), 0)
    prompt_lists = draw_prompt_lists(jax.random.fold_in(seeds[14], 71), 0)
    owner_map_keys = jax.random.split(jax.random.fold_in(seeds[5], 1), 2 * NBLK // NBLK)
    owner_map_turns = jax.random.permutation(jax.random.fold_in(seeds[5], 3), 2 * NBLK // NBLK)
    owner_map = jax.vmap(lambda own, number: assign_block(jax.random.fold_in(seeds[5], 2), own, number, NBLK, N_CTX, 1, NEW_CAP, 2))(owner_map_keys, owner_map_turns).reshape((2, NBLK, 1))
    w_uk = centred(seeds[6], (H, NOPE, LAT), NOPE ** -0.5, 0.5, ((0, 4),))
    w_uv = centred(seeds[7], (H, LAT, VDIM), (LAT // 8) ** -0.5, 0.75, ((0, 4),))
    dec_nope = centred(seeds[8], (2, DROWS, H * NOPE), 1.0, 6.0, ((0, 2), (2, 4)))
    dec_rope = draw_dec_rope(jax.random.fold_in(seeds[14], 71), 0)
    store_latent = centred(seeds[10], (2, DREQ, PPR, BLK, LAT), 1.0, 6.0, ((0, 2), (2, 32)))
    store_rope = draw_store_rope(jax.random.fold_in(seeds[14], 71), 0)
    lengths = draw_lengths(jax.random.fold_in(seeds[14], 71), 0)
    page_lists = draw_page_lists(jax.random.fold_in(seeds[14], 71), 0)
    return dict(q_nope=q_nope, q_rope=q_rope, prompt_latent=prompt_latent, prompt_rope=prompt_rope, prompt_lists=prompt_lists, owner_map=owner_map, w_uk=w_uk, w_uv=w_uv, dec_nope=dec_nope, dec_rope=dec_rope, store_latent=store_latent, store_rope=store_rope, lengths=lengths, page_lists=page_lists)


def rounded(values):
    return lax.optimization_barrier(values.astype(jnp.bfloat16)).astype(jnp.float32)


def attend(query_latent, query_rotary, key_latent, key_rotary, allowed):
    score_scale = (NOPE + ROPE) ** -0.5
    scores = jnp.einsum('qhl,kl->qhk', query_latent, key_latent, precision=lax.Precision.HIGHEST)
    scores = scores + jnp.einsum('qhe,ke->qhk', query_rotary, key_rotary, precision=lax.Precision.HIGHEST)
    scores = scores * score_scale
    masked = jnp.where(allowed, scores, -jnp.inf)
    peak_score = jnp.max(masked, axis=-1, keepdims=True)
    weights = jnp.where(allowed, jnp.exp(masked - peak_score), 0.0)
    totals = jnp.sum(weights, axis=-1)
    mixture = jnp.einsum('qhk,kl->qhl', rounded(weights), key_latent, precision=lax.Precision.HIGHEST)
    return rounded(mixture / totals[..., None])


def prompt_group(nope_part, rotary_part, latent_part, key_rotary_part, lists_part, up_key, up_value):
    tokens = nope_part.shape[0]
    blocks = tokens // BLK
    latent_blocks = latent_part.astype(jnp.float32).reshape(blocks, BLK, LAT)
    rotary_blocks = key_rotary_part.astype(jnp.float32).reshape(blocks, BLK, ROPE)
    offsets = jnp.arange(BLK, dtype=jnp.int32)

    def one_block(block_index):
        first_token = (block_index * BLK).astype(jnp.int32)
        queries = lax.dynamic_slice_in_dim(nope_part, first_token, BLK, 0).astype(jnp.float32).reshape(BLK, H, NOPE)
        query_rotary = lax.dynamic_slice_in_dim(rotary_part, first_token, BLK, 0).astype(jnp.float32).reshape(BLK, H, ROPE)
        absorbed = rounded(jnp.einsum('thn,hnl->thl', queries, up_key, precision=lax.Precision.HIGHEST))
        listed_ids = lists_part[block_index]
        key_latent = latent_blocks[listed_ids].reshape(TOPK * BLK, LAT)
        key_rotary = rotary_blocks[listed_ids].reshape(TOPK * BLK, ROPE)
        key_places = (listed_ids[:, None] * BLK + offsets[None, :]).reshape(TOPK * BLK)
        query_places = first_token + offsets
        allowed = (key_places[None, :] <= query_places[:, None])[:, None, :]
        mixture = attend(absorbed, query_rotary, key_latent, key_rotary, allowed)
        result = jnp.einsum('thl,hlv->thv', mixture, up_value, precision=lax.Precision.HIGHEST)
        return result.astype(jnp.bfloat16).reshape(BLK, H * VDIM)

    outputs = lax.map(one_block, jnp.arange(blocks, dtype=jnp.int32))
    return outputs.reshape(tokens, H * VDIM)


def decode_group(nope_part, rotary_part, cache_latent, cache_rotary, lengths_part, lists_part, up_key, up_value):
    offsets = jnp.arange(BLK, dtype=jnp.int32)

    def one_request(request):
        first_row = (request * ROWS_REQ).astype(jnp.int32)
        queries = lax.dynamic_slice_in_dim(nope_part, first_row, ROWS_REQ, 0).astype(jnp.float32).reshape(ROWS_REQ, H, NOPE)
        query_rotary = lax.dynamic_slice_in_dim(rotary_part, first_row, ROWS_REQ, 0).astype(jnp.float32).reshape(ROWS_REQ, H, ROPE)
        absorbed = rounded(jnp.einsum('qhn,hnl->qhl', queries, up_key, precision=lax.Precision.HIGHEST))
        listed_ids = lists_part[request]
        key_latent = cache_latent[request][listed_ids].astype(jnp.float32).reshape(TOPK * BLK, LAT)
        key_rotary = cache_rotary[request][listed_ids].astype(jnp.float32).reshape(TOPK * BLK, ROPE)
        key_places = (listed_ids[:, None] * BLK + offsets[None, :]).reshape(TOPK * BLK)
        allowed = (key_places < lengths_part[request])[None, None, :]
        mixture = attend(absorbed, query_rotary, key_latent, key_rotary, allowed)
        result = jnp.einsum('qhl,hlv->qhv', mixture, up_value, precision=lax.Precision.HIGHEST)
        return result.astype(jnp.bfloat16).reshape(ROWS_REQ, H * VDIM)

    outputs = lax.map(one_request, jnp.arange(DREQ, dtype=jnp.int32))
    return outputs.reshape(DREQ * ROWS_REQ, H * VDIM)


def landing(latent_part, key_rotary_part, owners_part):
    blocks = owners_part.shape[0]
    owners = owners_part[:, 0]
    onehot = (owners[:, None] == jnp.arange(N_CTX, dtype=jnp.int32)[None, :]).astype(jnp.int32)
    ranking = jnp.sum((jnp.cumsum(onehot, axis=0, dtype=jnp.int32) - 1) * onehot, axis=1, dtype=jnp.int32)
    slot_index = owners * NEW_CAP + ranking
    chooser = (slot_index[None, :] == jnp.arange(N_CTX * NEW_CAP, dtype=jnp.int32)[:, None]).astype(jnp.float32)
    latent_pages = latent_part.astype(jnp.float32).reshape(blocks, BLK * LAT)
    rotary_pages = key_rotary_part.astype(jnp.float32).reshape(blocks, BLK * ROPE)
    landed_lat = jnp.dot(chooser, latent_pages, precision=lax.Precision.HIGHEST)
    landed_rot = jnp.dot(chooser, rotary_pages, precision=lax.Precision.HIGHEST)
    return landed_lat.astype(jnp.bfloat16).reshape(N_CTX * NEW_CAP, BLK, LAT), landed_rot.astype(jnp.bfloat16)


def reference(q_nope, q_rope, prompt_latent, prompt_rope, prompt_lists, owner_map, w_uk, w_uv, dec_nope, dec_rope, store_latent, store_rope, lengths, page_lists):
    up_key = w_uk.astype(jnp.float32)
    up_value = w_uv.astype(jnp.float32)
    prompt_outputs = []
    decode_outputs = []
    landed_lats = []
    landed_rots = []
    for group_index in range(2):
        source = 1 - group_index
        prompt_outputs.append(prompt_group(q_nope[group_index], q_rope[group_index], prompt_latent[group_index], prompt_rope[group_index], prompt_lists[group_index], up_key, up_value))
        decode_outputs.append(decode_group(dec_nope[group_index], dec_rope[group_index], store_latent[group_index], store_rope[group_index], lengths[group_index], page_lists[group_index], up_key, up_value))
        landed_lat, landed_rot = landing(prompt_latent[source], prompt_rope[source], owner_map[source])
        landed_lats.append(landed_lat)
        landed_rots.append(landed_rot)
    return (jnp.stack(prompt_outputs), jnp.stack(decode_outputs), jnp.stack(landed_lats), jnp.stack(landed_rots))
```

```python
import functools

import jax
import jax.numpy as jnp
from jax import lax
from jax.experimental import pallas as pl
from jax.experimental.pallas import tpu as pltpu
from jax.sharding import Mesh, PartitionSpec as P

NOPE = 128
ROPE = 64
LAT = 512
VDIM = 128
BLK = 64
TOPK = 16
WIDE = LAT + 128
KEYS = TOPK * BLK
FEAT = 128
RROWS = BLK // 8
PART = BLK + RROWS
SET = TOPK * PART
LOW = -1e30
SCALE = (NOPE + ROPE) ** (-0.5)
SCALE2 = SCALE * 1.4426950408889634
F32 = jnp.float32
BF16 = jnp.bfloat16
NT = (((1,), (1,)), ((), ()))


PARAMS = pltpu.CompilerParams(vmem_limit_bytes=60 * 1024 * 1024)


def iota(shape, dim):
    return lax.broadcasted_iota(jnp.int32, shape, dim)


def whole(array):
    return pl.BlockSpec(array.shape, lambda *_: (0,) * len(array.shape))


SMALL = pl.BlockSpec(memory_space=pltpu.SMEM)


def unpaired(pairs):
    row, column = iota((BLK, BLK // 2), 0), iota((BLK, BLK // 2), 1)
    spread = jnp.where(row // 2 == column, 1.0, 0.0).astype(BF16)
    twice = jnp.dot(spread, pairs, preferred_element_type=F32)
    odd = iota((BLK, 128), 0) % 2 == 1
    return jnp.where(odd, pltpu.roll(twice, ROPE, 1), twice)


def slice_kernel(lat_ref, rope_ref, out_ref):
    count = lat_ref.shape[1] // FEAT
    tokens = unpaired(rope_ref[...])
    lane = iota((RROWS, 128), 1)
    for q in range(count):
        low = tokens[2 * q * RROWS : (2 * q + 1) * RROWS]
        high = tokens[(2 * q + 1) * RROWS : (2 * q + 2) * RROWS]
        rope = jnp.where(lane < ROPE, low, pltpu.roll(high, ROPE, 1)).astype(BF16)
        for z in range(out_ref.shape[0] // count):
            out_ref[z * count + q, :BLK] = lat_ref[:, q * FEAT : (q + 1) * FEAT]
            out_ref[z * count + q, BLK:] = rope


def slices(latent, rope, copies):
    out = jax.ShapeDtypeStruct((copies, PART, FEAT), BF16)
    return pl.pallas_call(
        slice_kernel,
        out_shape=out,
        grid=(1,),
        in_specs=[whole(latent), whole(rope)],
        out_specs=whole(out),
        compiler_params=PARAMS,
        name="slices",
    )(latent, rope)


def select_kernel(layout, code_ref, own_ref, near_ref, far_ref, back_ref, *refs):
    out_refs, all_ref = refs[:-1], refs[-1]
    start = 0
    for ref in (own_ref, near_ref, far_ref, back_ref):
        all_ref[start : start + ref.shape[0]] = ref[...]
        start += ref.shape[0]
    place = 0
    for sets, out_ref in zip(layout, out_refs):
        first = 0
        for blocks in sets:
            for j in range(0, blocks, 2):
                tails = []
                for i in (j, j + 1):
                    code = code_ref[place]
                    place += 1
                    source = jnp.maximum(code, 0)
                    lat = all_ref[source, :BLK]
                    tail = all_ref[source, BLK:].astype(F32)
                    if blocks < TOPK:
                        lat = jnp.where(code >= 0, lat, jnp.zeros_like(lat))
                        tail = jnp.where(code >= 0, tail, jnp.zeros_like(tail))
                    out_ref[first + i * BLK : first + (i + 1) * BLK] = lat
                    tails.append(tail)
                base = first + blocks * BLK + j * RROWS
                out_ref[base : base + 2 * RROWS] = jnp.concatenate(tails, axis=0).astype(BF16)
            first += blocks * PART


def select(codes, gathered, layout):
    sources = sum(part.shape[0] for part in gathered)
    outs = [jax.ShapeDtypeStruct((sum(sets) * PART, FEAT), BF16) for sets in layout]
    return pl.pallas_call(
        functools.partial(select_kernel, layout),
        out_shape=outs,
        grid=(1,),
        in_specs=[SMALL] + [whole(part) for part in gathered],
        out_specs=[whole(out) for out in outs],
        scratch_shapes=[pltpu.VMEM((sources, PART, FEAT), BF16)],
        compiler_params=PARAMS,
        name="select",
    )(codes, *gathered)


def quarter_of(me_ref, s):
    return lax.rem(me_ref[0] + 4 - me_ref[1] * s, 4)


def place_ropes(ref, quarter, rows):
    flat = rows.reshape(-1, 128)
    ref[:, 2 * quarter] = rows
    ref[:, 2 * quarter + 1] = pltpu.roll(flat, ROPE, 1).reshape(rows.shape)


def land_kernel(me_ref, *refs):
    parts = refs[:4]
    lat_ref, rope_ref, token_ref = refs[4:]
    slots = lat_ref.shape[0]
    for s, ref in enumerate(parts):
        q = quarter_of(me_ref, s)
        lat_ref[:, :, pl.ds(pl.multiple_of(q * FEAT, FEAT), FEAT)] = ref[: slots * BLK].reshape(
            slots, BLK, FEAT
        )
        place_ropes(token_ref, q, ref[slots * BLK :].astype(F32).reshape(slots, RROWS, 128))
    lane = iota((slots, 128), 1)
    for r in range(BLK // 2):
        octet, row = 2 * r // 8, 2 * r % 8
        even, odd = token_ref[:, octet, row, :], token_ref[:, octet, row + 1, :]
        both = jnp.where(lane < ROPE, even, pltpu.roll(odd, ROPE, 1))
        rope_ref[:, r * 128 : (r + 1) * 128] = both.astype(BF16)


def land(me, parts, slots):
    rows = slots * PART
    outs = (
        jax.ShapeDtypeStruct((slots, BLK, LAT), BF16),
        jax.ShapeDtypeStruct((slots, BLK * ROPE), BF16),
    )
    return pl.pallas_call(
        land_kernel,
        out_shape=outs,
        grid=(1,),
        in_specs=[SMALL] + [pl.BlockSpec((rows, FEAT), lambda c: (SET // rows, 0))] * len(parts),
        out_specs=tuple(whole(out) for out in outs),
        scratch_shapes=[pltpu.VMEM((slots, 8, 8, 128), F32)],
        compiler_params=PARAMS,
        name="land",
    )(me, *parts)


def split_kernel(me_ref, nope_ref, rope_ref, *out_refs):
    count = len(out_refs)
    nope, rope = nope_ref.shape[1] // count, rope_ref.shape[1] // count
    for s, out_ref in enumerate(out_refs):
        to = lax.rem(me_ref[0] + s, count)
        out_ref[:, :nope] = nope_ref[:, pl.ds(pl.multiple_of(to * nope, 128), nope)]
        out_ref[:, nope:] = rope_ref[:, pl.ds(pl.multiple_of(to * rope, 128), rope)]


def split(me, nope, rope, count):
    out = jax.ShapeDtypeStruct((nope.shape[0], (nope.shape[1] + rope.shape[1]) // count), BF16)
    return pl.pallas_call(
        split_kernel,
        out_shape=[out] * count,
        grid=(1,),
        in_specs=[SMALL, whole(nope), whole(rope)],
        out_specs=[whole(out)] * count,
        cost_estimate=pl.CostEstimate(
            flops=0, bytes_accessed=4 * (nope.size + rope.size), transcendentals=0
        ),
        compiler_params=PARAMS,
        name="split",
    )(me, nope, rope)


def absorb_kernel(order_ref, *refs):
    wuk_ref, out_ref = refs[-2:]
    blocks = out_ref.shape[0]
    nope = jnp.concatenate([ref[...] for ref in refs[:blocks]], axis=0)
    rope = jnp.concatenate([ref[...] for ref in refs[blocks : 2 * blocks]], axis=0).astype(F32)
    lane = iota((blocks * BLK, 128), 1)
    spot = iota((blocks * BLK, 128), 0) % BLK
    onehot = jnp.where(lane == spot + ROPE, 1.0, 0.0)
    for i in range(wuk_ref.shape[0]):
        part = rope[:, i // 2 * 128 : i // 2 * 128 + 128]
        if i % 2 == 1:
            part = pltpu.roll(part, ROPE, 1)
        tail = jnp.where(lane < ROPE, part, onehot).astype(BF16)
        absorbed = jnp.dot(
            nope[:, i * NOPE : (i + 1) * NOPE], wuk_ref[i], preferred_element_type=F32
        ).astype(BF16)
        rows = slice(i * BLK, (i + 1) * BLK)
        for b in range(blocks):
            out_ref[order_ref[b], rows, :LAT] = absorbed[b * BLK : (b + 1) * BLK]
            out_ref[order_ref[b], rows, LAT:] = tail[b * BLK : (b + 1) * BLK]


def absorb(order, queries, w_uk):
    blocks = len(queries)
    heads = w_uk.shape[0]
    some = 4
    rows = blocks * BLK * heads
    nope_spec = pl.BlockSpec((BLK, some * NOPE), lambda p: (0, p))
    rope_spec = pl.BlockSpec((BLK, some * ROPE), lambda p: (0, p + heads * NOPE // (some * ROPE)))
    return pl.pallas_call(
        absorb_kernel,
        out_shape=jax.ShapeDtypeStruct((blocks, heads * BLK, WIDE), BF16),
        grid=(heads // some,),
        in_specs=[SMALL]
        + [nope_spec] * blocks
        + [rope_spec] * blocks
        + [pl.BlockSpec((some, NOPE, LAT), lambda p: (p, 0, 0))],
        out_specs=pl.BlockSpec((blocks, some * BLK, WIDE), lambda p: (0, p, 0)),
        cost_estimate=pl.CostEstimate(
            flops=2 * rows * NOPE * LAT,
            bytes_accessed=rows * (WIDE + 192) * 2 + heads * NOPE * LAT * 2,
            transcendentals=0,
        ),
        compiler_params=PARAMS,
        name="absorb",
    )(order, *queries, *queries, w_uk)


def attend_kernel(mixed, ids_ref, block_ref, me_ref, *refs):
    set_refs, q_ref, refs = refs[:4], refs[4], refs[4:]
    mix_refs, wuv_ref = refs[1 : 1 + mixed], refs[-4]
    out_ref, keys_ref, token_ref = refs[-3:]

    @pl.when(pl.program_id(0) == 0)
    def _():
        for s, ref in enumerate(set_refs):
            quarter = quarter_of(me_ref, s)
            keys_ref[:, pl.ds(pl.multiple_of(quarter * FEAT, FEAT), FEAT)] = ref[:KEYS]
            place_ropes(token_ref, quarter, ref[KEYS:].astype(F32).reshape(TOPK, RROWS, 128))
        lane = iota((BLK, 128), 1)
        row = iota((BLK, 128), 0)
        place = block_ref[0] * BLK
        for j in range(TOPK):
            late = row + ids_ref[j] * BLK > place + lane - ROPE
            bias = jnp.where(late, LOW, 0.0)
            tail = jnp.where(lane < ROPE, token_ref[j].reshape(BLK, 128), bias)
            keys_ref[j * BLK : (j + 1) * BLK, LAT:] = tail.astype(BF16)

    rows = 4 * BLK
    chunks = [slice(at, at + rows) for at in range(0, q_ref.shape[1], rows)]
    scores = [
        lax.dot_general(q_ref[0, chunk, :], keys_ref[...], NT, preferred_element_type=F32)
        for chunk in chunks
    ]
    for chunk, s in zip(chunks, scores):
        peak = jnp.max(s, axis=1, keepdims=True)
        w = jnp.exp2((s - peak) * SCALE2)
        total = jnp.sum(w, axis=1, keepdims=True)
        o = jnp.dot(w.astype(BF16), keys_ref[:, :LAT], preferred_element_type=F32)
        o = (o * (1.0 / total)).astype(BF16)
        if mixed == 0:
            out_ref[chunk] = o
            continue
        for i in range(rows // BLK):
            h = chunk.start // BLK + i
            here = slice(h * BLK, (h + 1) * BLK)
            mixture = jnp.concatenate(
                [ref[here] for ref in mix_refs] + [o[i * BLK : (i + 1) * BLK]], axis=0
            )
            out_ref[:, h * VDIM : (h + 1) * VDIM] = jnp.dot(
                mixture, wuv_ref[h], preferred_element_type=F32
            ).astype(BF16)


def attend(index, sets, ids, block, me, q, mixtures=(), w_uv=None):
    rows = q.shape[1]
    steps = 2
    some = rows // steps
    operands = [ids, block, me, *sets, q]
    in_specs = (
        [SMALL] * 3
        + [pl.BlockSpec((SET, FEAT), lambda c: (0, 0))] * len(sets)
        + [pl.BlockSpec((1, some, WIDE), lambda c: (index, c, 0))]
    )
    if mixtures:
        tokens, heads = (len(mixtures) + 1) * BLK, w_uv.shape[0]
        operands += [*mixtures, w_uv]
        in_specs += [pl.BlockSpec((some, LAT), lambda c: (c, 0))] * len(mixtures)
        in_specs.append(pl.BlockSpec((heads // steps, LAT, VDIM), lambda c: (c, 0, 0)))
        out_shape = jax.ShapeDtypeStruct((tokens, heads * VDIM), BF16)
        out_spec = pl.BlockSpec((tokens, heads // steps * VDIM), lambda c: (0, c))
    else:
        out_shape = jax.ShapeDtypeStruct((rows, LAT), BF16)
        out_spec = pl.BlockSpec((some, LAT), lambda c: (c, 0))
    return pl.pallas_call(
        functools.partial(attend_kernel, len(mixtures)),
        out_shape=out_shape,
        grid=(steps,),
        in_specs=in_specs,
        out_specs=out_spec,
        scratch_shapes=[pltpu.VMEM((KEYS, WIDE), BF16), pltpu.VMEM((TOPK, 8, 8, 128), F32)],
        cost_estimate=pl.CostEstimate(
            flops=2 * rows * KEYS * (WIDE + LAT),
            bytes_accessed=rows * (WIDE + LAT) * 2 + 4 * SET * FEAT * 2,
            transcendentals=rows * KEYS,
        ),
        compiler_params=PARAMS,
        name="attend",
    )(*operands)


def decode_kernel(pages_ref, len_ref, first_ref, nope_ref, rope_ref, wuk_ref, wuv_ref,
                  lat_ref, keyrope_ref, out_ref, q_ref, mix_ref, stat_ref):
    heads = wuk_ref.shape[0]
    rows_total = nope_ref.shape[0]
    requests, pages = lat_ref.shape[0], lat_ref.shape[1]
    each = rows_total // requests
    local = pages * BLK
    lane = iota((rows_total, 128), 1)
    for h in range(heads):
        pair = rope_ref[:, h // 2 * 128 : h // 2 * 128 + 128].astype(F32)
        if h % 2 == 1:
            pair = pltpu.roll(pair, ROPE, 1)
        absorbed = jnp.dot(
            nope_ref[:, h * NOPE : (h + 1) * NOPE], wuk_ref[h], preferred_element_type=F32
        ).astype(BF16)
        tail = jnp.where(lane < ROPE, pair, 0.0).astype(BF16)
        for r in range(requests):
            q_ref[r, h * each : (h + 1) * each, :LAT] = absorbed[r * each : (r + 1) * each]
            q_ref[r, h * each : (h + 1) * each, LAT:] = tail[r * each : (r + 1) * each]
    first = first_ref[0]
    key_lane = iota((1, local), 1)
    for r in range(requests):
        usable = jnp.zeros((1, local), jnp.int32)
        for p in range(pages):
            page = first + p
            listed = pages_ref[r, 0] == page
            for j in range(1, pages_ref.shape[1]):
                listed = jnp.logical_or(listed, pages_ref[r, j] == page)
            filled = jnp.where(listed, jnp.clip(len_ref[r] - page * BLK, 0, BLK), 0)
            inside = (key_lane >= p * BLK) & (key_lane < p * BLK + filled)
            usable = jnp.where(inside, 1, usable)
        keep = usable > 0
        lat = lat_ref[r].reshape(local, LAT)
        tails = jnp.concatenate(
            [unpaired(keyrope_ref[r, p]) for p in range(pages)], axis=0
        )
        tails = jnp.where(iota((local, 128), 1) < ROPE, tails, 0.0).astype(BF16)
        s = lax.dot_general(q_ref[r, :, :LAT], lat, NT, preferred_element_type=F32)
        s = s + lax.dot_general(q_ref[r, :, LAT:], tails, NT, preferred_element_type=F32)
        s = jnp.where(keep, s, LOW)
        peak = jnp.max(s, axis=1, keepdims=True)
        peak_hi = peak.astype(BF16).astype(F32)
        peak_lo = (peak - peak_hi).astype(BF16).astype(F32)
        w = jnp.where(keep, jnp.exp2((s - (peak_hi + peak_lo)) * SCALE2), 0.0)
        total = jnp.sum(w, axis=1, keepdims=True)
        total_hi = total.astype(BF16).astype(F32)
        total_lo = total - total_hi
        o = jnp.dot(w.astype(BF16), lat, preferred_element_type=F32).astype(BF16)
        stat_lane = iota((heads * each, 128), 1)
        stat = jnp.where(stat_lane < 2 * heads, peak_hi, total_hi)
        low = jnp.where(stat_lane < 2 * heads, peak_lo, total_lo)
        stat = jnp.where(stat_lane % (2 * heads) < heads, stat, low)
        for h in range(heads):
            mix_ref[h, r * each : (r + 1) * each, :] = o[h * each : (h + 1) * each]
        merged = jnp.zeros((each, 128), F32)
        for h in range(heads):
            here = iota((each, 128), 1) % heads == h
            merged = jnp.where(here, stat[h * each : (h + 1) * each], merged)
        stat_ref[r * each : (r + 1) * each, :] = merged
    for h in range(heads):
        out_ref[:, h * VDIM : (h + 1) * VDIM] = jnp.dot(
            mix_ref[h], wuv_ref[h], preferred_element_type=F32
        ).astype(BF16)
    out_ref[:, heads * VDIM :] = stat_ref[...].astype(BF16)


def decode(page_lists, lengths, first, nope, rope, w_uk, w_uv, latents, ropes):
    rows = nope.shape[0]
    heads = w_uk.shape[0]
    requests = latents.shape[0]
    each = rows // requests
    operands = (nope, rope, w_uk, w_uv, latents, ropes)
    out = jax.ShapeDtypeStruct((rows, heads * VDIM + 128), BF16)
    return pl.pallas_call(
        decode_kernel,
        out_shape=out,
        grid=(1,),
        in_specs=[SMALL] * 3 + [whole(operand) for operand in operands],
        out_specs=whole(out),
        scratch_shapes=[
            pltpu.VMEM((requests, heads * each, WIDE), BF16),
            pltpu.VMEM((heads, rows, LAT), BF16),
            pltpu.VMEM((rows, 128), F32),
        ],
        cost_estimate=pl.CostEstimate(
            flops=1000000000, bytes_accessed=7 * 1024 * 1024, transcendentals=300000
        ),
        compiler_params=PARAMS,
        name="decode",
    )(page_lists, lengths, first, *operands)


def combine_kernel(parts_ref, out_ref):
    sources, rows = parts_ref.shape[0], parts_ref.shape[1]
    width = out_ref.shape[1]
    heads = width // VDIM
    for row in range(rows):
        part = parts_ref[:, row, :].astype(F32)
        stat = part[:, width:]
        peak = stat[:, :heads] + stat[:, heads : 2 * heads]
        total = stat[:, 2 * heads : 3 * heads] + stat[:, 3 * heads : 4 * heads]
        top = jnp.max(peak, axis=0, keepdims=True)
        factor = jnp.exp2((peak - top) * SCALE2)
        factor = factor / jnp.sum(factor * total, axis=0, keepdims=True)
        for h in range(heads):
            value = part[:, h * VDIM : (h + 1) * VDIM] * factor[:, h : h + 1]
            out_ref[row : row + 1, h * VDIM : (h + 1) * VDIM] = jnp.sum(
                value, axis=0, keepdims=True
            ).astype(BF16)


def combine(parts, width):
    out = jax.ShapeDtypeStruct((parts.shape[1], width), BF16)
    return pl.pallas_call(
        combine_kernel,
        out_shape=out,
        grid=(1,),
        in_specs=[whole(parts)],
        out_specs=whole(out),
        compiler_params=PARAMS,
        name="combine",
    )(parts)


def shifted(block, axis, distance):
    count = lax.axis_size(axis)
    return lax.ppermute(block, axis, [(i, (i + distance) % count) for i in range(count)])


def turned(block, axis, distance):
    count = lax.axis_size(axis)
    route = [
        (g * count + i, g * count + (i + (distance, -distance)[g]) % count)
        for g in (0, 1)
        for i in range(count)
    ]
    return lax.ppermute(block, ("grp", axis), route)


CTX = ("y", "z")


def after(value, *earlier):
    return lax.optimization_barrier((value, *earlier))[0]


def body(
    q_nope,
    q_rope,
    prompt_latent,
    prompt_rope,
    prompt_lists,
    owner_map,
    w_uk,
    w_uv,
    dec_nope,
    dec_rope,
    store_latent,
    store_rope,
    lengths,
    page_lists,
):
    y, z, me = lax.axis_index("y"), lax.axis_index("z"), lax.axis_index("hd")
    ys, zs, count = lax.axis_size("y"), lax.axis_size("z"), lax.axis_size("hd")
    ctx, contexts = y * zs + z, ys * zs
    block_count = contexts * count
    query_blocks = count
    turn = 1 - 2 * lax.axis_index("grp")
    here = me.reshape(1)
    ring = jnp.stack([me, turn])

    chunk = slices(prompt_latent[0], prompt_rope[0], zs * count)
    chunk = lax.all_to_all(chunk, ("z", "hd"), split_axis=0, concat_axis=0, tiled=True)

    requests, per_device = store_latent.shape[1], store_latent.shape[2]
    parts = decode(
        page_lists[0],
        lengths[0],
        (ctx * per_device).reshape(1),
        dec_nope[0],
        dec_rope[0],
        w_uk,
        w_uv,
        store_latent[0],
        store_rope[0].reshape(requests, per_device, BLK // 2, 128),
    )
    rows_total, wide = parts.shape
    parts = parts.reshape(contexts, rows_total // contexts, wide)

    shares = split(here, q_nope[0], q_rope[0], count)
    hop = turned(shares[2], "hd", 1)
    queries = [shares[0], shifted(shares[1], "hd", 1), None, shifted(shares[3], "hd", 3)]
    chunk = after(chunk, parts, hop, queries[1], queries[3])
    queries[2] = turned(hop, "hd", 1)
    near, back = turned(chunk, "y", 1), turned(chunk, "y", -1)
    far = turned(near, "y", 1)

    order = (me - jnp.arange(query_blocks, dtype=jnp.int32)) % count
    q = absorb(order, queries, w_uk)

    first_block = ctx * query_blocks
    listed = lax.dynamic_slice_in_dim(prompt_lists[0], first_block, query_blocks, 0)
    slot_count = 2 * block_count // contexts
    mine = (owner_map[0, :, 0] == ctx).astype(jnp.int32)
    ranking = jnp.cumsum(mine) - 1
    hit = (mine[None, :] == 1) & (
        ranking[None, :] == jnp.arange(slot_count, dtype=jnp.int32)[:, None]
    )
    pages = jnp.max(
        jnp.where(hit, jnp.arange(block_count, dtype=jnp.int32)[None, :], -1), axis=1
    )
    carrier = 2
    layout = [(TOPK,)] * query_blocks
    layout[carrier] = (TOPK, slot_count)
    wanted = jnp.concatenate(
        [listed[: carrier + 1].reshape(-1), pages, listed[carrier + 1 :].reshape(-1)]
    )
    row = zs * count
    codes = turn * (y - wanted // row) % ys * row + wanted % row
    codes = jnp.where(wanted < 0, -1, codes)

    parts = lax.all_to_all(parts, CTX, split_axis=0, concat_axis=0, tiled=True)
    dec_out = combine(parts, w_uv.shape[0] * VDIM)
    codes = after(codes, q, dec_out)
    sets = select(codes, (chunk, near, far, back), tuple(layout))

    rings, mixtures = [], []

    def mix(index, *ready):
        ids = after(listed[index], *ready)
        at = (first_block + index).reshape(1)
        mixtures.append(attend(index, rings[index], ids, at, ring, q))

    near_sets = []
    for index, block in enumerate(sets):
        if index >= 2:
            block = after(block, *near_sets[index - 2])
        near_sets.append((turned(block, "hd", 1), turned(block, "hd", -1)))
    for index, block in enumerate(sets):
        ahead, behind = near_sets[index]
        earlier = [rings[-1][2], mixtures[-1]] if index >= 2 else []
        far = turned(after(ahead, behind, *earlier), "hd", 1)
        rings.append((block, ahead, far, behind))
        if index in (1, 2):
            mix(index - 1, *near_sets[1])
    mix(2, mixtures[-1], *near_sets[3])
    landed = land(after(ring, mixtures[-1], rings[-1][2]), rings[carrier], slot_count)
    landed_latent, landed_rope = (lax.ppermute(x, "grp", [(0, 1), (1, 0)]) for x in landed)
    last = query_blocks - 1
    at = (first_block + last).reshape(1)
    pre_out = attend(last, rings[last], listed[last], at, ring, q, mixtures, w_uv)
    return (pre_out[None], dec_out[None], landed_latent[None], landed_rope[None])


def solution(mesh):
    mesh = Mesh(mesh.devices.reshape(2, 4, 8, 4), ("grp", *CTX, "hd"))
    in_specs = (
        P("grp", (*CTX, "hd"), None),
        P("grp", (*CTX, "hd"), None),
        P("grp", (*CTX, "hd"), None),
        P("grp", (*CTX, "hd"), None),
        P("grp", None, None),
        P("grp", None, None),
        P("hd", None, None),
        P("hd", None, None),
        P("grp", None, "hd"),
        P("grp", None, "hd"),
        P("grp", None, CTX, None, None),
        P("grp", None, CTX, None),
        P("grp", None),
        P("grp", None, None),
    )
    out_specs = (
        P("grp", CTX, "hd"),
        P("grp", CTX, "hd"),
        P("grp", CTX, None, None),
        P("grp", CTX, None),
    )
    return jax.shard_map(body, mesh=mesh, in_specs=in_specs, out_specs=out_specs, check_vma=False)
```

```python
import functools

import jax
import jax.numpy as jnp
from jax import lax
from jax.experimental import pallas as pl
from jax.experimental.pallas import tpu as pltpu
from jax.sharding import Mesh, PartitionSpec as P

NOPE = 128
ROPE = 64
LAT = 512
VDIM = 128
BLK = 64
TOPK = 16
WIDE = LAT + 128
KEYS = TOPK * BLK
FEAT = 128
RROWS = BLK // 8
PART = BLK + RROWS
SET = TOPK * PART
LOW = -1e30
SCALE = (NOPE + ROPE) ** (-0.5)
SCALE2 = SCALE * 1.4426950408889634
F32 = jnp.float32
BF16 = jnp.bfloat16
NT = (((1,), (1,)), ((), ()))


PARAMS = pltpu.CompilerParams(vmem_limit_bytes=60 * 1024 * 1024)


def iota(shape, dim):
    return lax.broadcasted_iota(jnp.int32, shape, dim)


def whole(array):
    return pl.BlockSpec(array.shape, lambda *_: (0,) * len(array.shape))


SMALL = pl.BlockSpec(memory_space=pltpu.SMEM)


def unpaired(pairs):
    row, column = iota((BLK, BLK // 2), 0), iota((BLK, BLK // 2), 1)
    spread = jnp.where(row // 2 == column, 1.0, 0.0).astype(BF16)
    twice = jnp.dot(spread, pairs, preferred_element_type=F32)
    odd = iota((BLK, 128), 0) % 2 == 1
    return jnp.where(odd, pltpu.roll(twice, ROPE, 1), twice)


def slice_kernel(lat_ref, rope_ref, out_ref):
    count = lat_ref.shape[1] // FEAT
    tokens = unpaired(rope_ref[...])
    lane = iota((RROWS, 128), 1)
    for q in range(count):
        low = tokens[2 * q * RROWS : (2 * q + 1) * RROWS]
        high = tokens[(2 * q + 1) * RROWS : (2 * q + 2) * RROWS]
        rope = jnp.where(lane < ROPE, low, pltpu.roll(high, ROPE, 1)).astype(BF16)
        for z in range(out_ref.shape[0] // count):
            out_ref[z * count + q, :BLK] = lat_ref[:, q * FEAT : (q + 1) * FEAT]
            out_ref[z * count + q, BLK:] = rope


def slices(latent, rope, copies):
    out = jax.ShapeDtypeStruct((copies, PART, FEAT), BF16)
    return pl.pallas_call(
        slice_kernel,
        out_shape=out,
        grid=(1,),
        in_specs=[whole(latent), whole(rope)],
        out_specs=whole(out),
        compiler_params=PARAMS,
        name="slices",
    )(latent, rope)


def select_kernel(layout, code_ref, own_ref, near_ref, far_ref, back_ref, *refs):
    out_refs, all_ref = refs[:-1], refs[-1]
    start = 0
    for ref in (own_ref, near_ref, far_ref, back_ref):
        all_ref[start : start + ref.shape[0]] = ref[...]
        start += ref.shape[0]
    place = 0
    for sets, out_ref in zip(layout, out_refs):
        first = 0
        for blocks in sets:
            for j in range(0, blocks, 2):
                tails = []
                for i in (j, j + 1):
                    code = code_ref[place]
                    place += 1
                    source = jnp.maximum(code, 0)
                    lat = all_ref[source, :BLK]
                    tail = all_ref[source, BLK:].astype(F32)
                    if blocks < TOPK:
                        lat = jnp.where(code >= 0, lat, jnp.zeros_like(lat))
                        tail = jnp.where(code >= 0, tail, jnp.zeros_like(tail))
                    out_ref[first + i * BLK : first + (i + 1) * BLK] = lat
                    tails.append(tail)
                base = first + blocks * BLK + j * RROWS
                out_ref[base : base + 2 * RROWS] = jnp.concatenate(tails, axis=0).astype(BF16)
            first += blocks * PART


def select(codes, gathered, layout):
    sources = sum(part.shape[0] for part in gathered)
    outs = [jax.ShapeDtypeStruct((sum(sets) * PART, FEAT), BF16) for sets in layout]
    return pl.pallas_call(
        functools.partial(select_kernel, layout),
        out_shape=outs,
        grid=(1,),
        in_specs=[SMALL] + [whole(part) for part in gathered],
        out_specs=[whole(out) for out in outs],
        scratch_shapes=[pltpu.VMEM((sources, PART, FEAT), BF16)],
        compiler_params=PARAMS,
        name="select",
    )(codes, *gathered)


def quarter_of(me_ref, s):
    return lax.rem(me_ref[0] + 4 - me_ref[1] * s, 4)


def place_ropes(ref, quarter, rows):
    flat = rows.reshape(-1, 128)
    ref[:, 2 * quarter] = rows
    ref[:, 2 * quarter + 1] = pltpu.roll(flat, ROPE, 1).reshape(rows.shape)


def land_kernel(me_ref, *refs):
    parts = refs[:4]
    lat_ref, rope_ref, token_ref = refs[4:]
    slots = lat_ref.shape[0]
    for s, ref in enumerate(parts):
        q = quarter_of(me_ref, s)
        lat_ref[:, :, pl.ds(pl.multiple_of(q * FEAT, FEAT), FEAT)] = ref[: slots * BLK].reshape(
            slots, BLK, FEAT
        )
        place_ropes(token_ref, q, ref[slots * BLK :].astype(F32).reshape(slots, RROWS, 128))
    lane = iota((slots, 128), 1)
    for r in range(BLK // 2):
        octet, row = 2 * r // 8, 2 * r % 8
        even, odd = token_ref[:, octet, row, :], token_ref[:, octet, row + 1, :]
        both = jnp.where(lane < ROPE, even, pltpu.roll(odd, ROPE, 1))
        rope_ref[:, r * 128 : (r + 1) * 128] = both.astype(BF16)


def land(me, parts, slots):
    rows = slots * PART
    outs = (
        jax.ShapeDtypeStruct((slots, BLK, LAT), BF16),
        jax.ShapeDtypeStruct((slots, BLK * ROPE), BF16),
    )
    return pl.pallas_call(
        land_kernel,
        out_shape=outs,
        grid=(1,),
        in_specs=[SMALL] + [pl.BlockSpec((rows, FEAT), lambda c: (SET // rows, 0))] * len(parts),
        out_specs=tuple(whole(out) for out in outs),
        scratch_shapes=[pltpu.VMEM((slots, 8, 8, 128), F32)],
        compiler_params=PARAMS,
        name="land",
    )(me, *parts)


def split_kernel(me_ref, nope_ref, rope_ref, *out_refs):
    count = len(out_refs)
    nope, rope = nope_ref.shape[1] // count, rope_ref.shape[1] // count
    for s, out_ref in enumerate(out_refs):
        to = lax.rem(me_ref[0] + s, count)
        out_ref[:, :nope] = nope_ref[:, pl.ds(pl.multiple_of(to * nope, 128), nope)]
        out_ref[:, nope:] = rope_ref[:, pl.ds(pl.multiple_of(to * rope, 128), rope)]


def split(me, nope, rope, count):
    out = jax.ShapeDtypeStruct((nope.shape[0], (nope.shape[1] + rope.shape[1]) // count), BF16)
    return pl.pallas_call(
        split_kernel,
        out_shape=[out] * count,
        grid=(1,),
        in_specs=[SMALL, whole(nope), whole(rope)],
        out_specs=[whole(out)] * count,
        cost_estimate=pl.CostEstimate(
            flops=0, bytes_accessed=4 * (nope.size + rope.size), transcendentals=0
        ),
        compiler_params=PARAMS,
        name="split",
    )(me, nope, rope)


def absorb_kernel(order_ref, *refs):
    wuk_ref, out_ref = refs[-2:]
    blocks = out_ref.shape[0]
    nope = jnp.concatenate([ref[...] for ref in refs[:blocks]], axis=0)
    rope = jnp.concatenate([ref[...] for ref in refs[blocks : 2 * blocks]], axis=0).astype(F32)
    lane = iota((blocks * BLK, 128), 1)
    spot = iota((blocks * BLK, 128), 0) % BLK
    onehot = jnp.where(lane == spot + ROPE, 1.0, 0.0)
    for i in range(wuk_ref.shape[0]):
        part = rope[:, i // 2 * 128 : i // 2 * 128 + 128]
        if i % 2 == 1:
            part = pltpu.roll(part, ROPE, 1)
        tail = jnp.where(lane < ROPE, part, onehot).astype(BF16)
        absorbed = jnp.dot(
            nope[:, i * NOPE : (i + 1) * NOPE], wuk_ref[i], preferred_element_type=F32
        ).astype(BF16)
        rows = slice(i * BLK, (i + 1) * BLK)
        for b in range(blocks):
            out_ref[order_ref[b], rows, :LAT] = absorbed[b * BLK : (b + 1) * BLK]
            out_ref[order_ref[b], rows, LAT:] = tail[b * BLK : (b + 1) * BLK]


def absorb(order, queries, w_uk):
    blocks = len(queries)
    heads = w_uk.shape[0]
    some = 4
    rows = blocks * BLK * heads
    nope_spec = pl.BlockSpec((BLK, some * NOPE), lambda p: (0, p))
    rope_spec = pl.BlockSpec((BLK, some * ROPE), lambda p: (0, p + heads * NOPE // (some * ROPE)))
    return pl.pallas_call(
        absorb_kernel,
        out_shape=jax.ShapeDtypeStruct((blocks, heads * BLK, WIDE), BF16),
        grid=(heads // some,),
        in_specs=[SMALL]
        + [nope_spec] * blocks
        + [rope_spec] * blocks
        + [pl.BlockSpec((some, NOPE, LAT), lambda p: (p, 0, 0))],
        out_specs=pl.BlockSpec((blocks, some * BLK, WIDE), lambda p: (0, p, 0)),
        cost_estimate=pl.CostEstimate(
            flops=2 * rows * NOPE * LAT,
            bytes_accessed=rows * (WIDE + 192) * 2 + heads * NOPE * LAT * 2,
            transcendentals=0,
        ),
        compiler_params=PARAMS,
        name="absorb",
    )(order, *queries, *queries, w_uk)


def attend_kernel(mixed, ids_ref, block_ref, me_ref, *refs):
    set_refs, q_ref, refs = refs[:4], refs[4], refs[4:]
    mix_refs, wuv_ref = refs[1 : 1 + mixed], refs[-4]
    out_ref, keys_ref, token_ref = refs[-3:]

    @pl.when(pl.program_id(0) == 0)
    def _():
        for s, ref in enumerate(set_refs):
            quarter = quarter_of(me_ref, s)
            keys_ref[:, pl.ds(pl.multiple_of(quarter * FEAT, FEAT), FEAT)] = ref[:KEYS]
            place_ropes(token_ref, quarter, ref[KEYS:].astype(F32).reshape(TOPK, RROWS, 128))
        lane = iota((BLK, 128), 1)
        row = iota((BLK, 128), 0)
        place = block_ref[0] * BLK
        for j in range(TOPK):
            late = row + ids_ref[j] * BLK > place + lane - ROPE
            bias = jnp.where(late, LOW, 0.0)
            tail = jnp.where(lane < ROPE, token_ref[j].reshape(BLK, 128), bias)
            keys_ref[j * BLK : (j + 1) * BLK, LAT:] = tail.astype(BF16)

    rows = 4 * BLK
    chunks = [slice(at, at + rows) for at in range(0, q_ref.shape[1], rows)]
    scores = [
        lax.dot_general(q_ref[0, chunk, :], keys_ref[...], NT, preferred_element_type=F32)
        for chunk in chunks
    ]
    for chunk, s in zip(chunks, scores):
        peak = jnp.max(s, axis=1, keepdims=True)
        w = jnp.exp2((s - peak) * SCALE2)
        total = jnp.sum(w, axis=1, keepdims=True)
        o = jnp.dot(w.astype(BF16), keys_ref[:, :LAT], preferred_element_type=F32)
        o = (o * (1.0 / total)).astype(BF16)
        if mixed == 0:
            out_ref[chunk] = o
            continue
        for i in range(rows // BLK):
            h = chunk.start // BLK + i
            here = slice(h * BLK, (h + 1) * BLK)
            mixture = jnp.concatenate(
                [ref[here] for ref in mix_refs] + [o[i * BLK : (i + 1) * BLK]], axis=0
            )
            out_ref[:, h * VDIM : (h + 1) * VDIM] = jnp.dot(
                mixture, wuv_ref[h], preferred_element_type=F32
            ).astype(BF16)


def attend(index, sets, ids, block, me, q, mixtures=(), w_uv=None):
    rows = q.shape[1]
    steps = 2
    some = rows // steps
    operands = [ids, block, me, *sets, q]
    in_specs = (
        [SMALL] * 3
        + [pl.BlockSpec((SET, FEAT), lambda c: (0, 0))] * len(sets)
        + [pl.BlockSpec((1, some, WIDE), lambda c: (index, c, 0))]
    )
    if mixtures:
        tokens, heads = (len(mixtures) + 1) * BLK, w_uv.shape[0]
        operands += [*mixtures, w_uv]
        in_specs += [pl.BlockSpec((some, LAT), lambda c: (c, 0))] * len(mixtures)
        in_specs.append(pl.BlockSpec((heads // steps, LAT, VDIM), lambda c: (c, 0, 0)))
        out_shape = jax.ShapeDtypeStruct((tokens, heads * VDIM), BF16)
        out_spec = pl.BlockSpec((tokens, heads // steps * VDIM), lambda c: (0, c))
    else:
        out_shape = jax.ShapeDtypeStruct((rows, LAT), BF16)
        out_spec = pl.BlockSpec((some, LAT), lambda c: (c, 0))
    return pl.pallas_call(
        functools.partial(attend_kernel, len(mixtures)),
        out_shape=out_shape,
        grid=(steps,),
        in_specs=in_specs,
        out_specs=out_spec,
        scratch_shapes=[pltpu.VMEM((KEYS, WIDE), BF16), pltpu.VMEM((TOPK, 8, 8, 128), F32)],
        cost_estimate=pl.CostEstimate(
            flops=2 * rows * KEYS * (WIDE + LAT),
            bytes_accessed=rows * (WIDE + LAT) * 2 + 4 * SET * FEAT * 2,
            transcendentals=rows * KEYS,
        ),
        compiler_params=PARAMS,
        name="attend",
    )(*operands)


def decode_kernel(pages_ref, len_ref, first_ref, nope_ref, rope_ref, wuk_ref, wuv_ref,
                  lat_ref, keyrope_ref, out_ref, q_ref, mix_ref, stat_ref):
    heads = wuk_ref.shape[0]
    rows_total = nope_ref.shape[0]
    requests, pages = lat_ref.shape[0], lat_ref.shape[1]
    each = rows_total // requests
    local = pages * BLK
    lane = iota((rows_total, 128), 1)
    for h in range(heads):
        pair = rope_ref[:, h // 2 * 128 : h // 2 * 128 + 128].astype(F32)
        if h % 2 == 1:
            pair = pltpu.roll(pair, ROPE, 1)
        absorbed = jnp.dot(
            nope_ref[:, h * NOPE : (h + 1) * NOPE], wuk_ref[h], preferred_element_type=F32
        ).astype(BF16)
        tail = jnp.where(lane < ROPE, pair, 0.0).astype(BF16)
        for r in range(requests):
            q_ref[r, h * each : (h + 1) * each, :LAT] = absorbed[r * each : (r + 1) * each]
            q_ref[r, h * each : (h + 1) * each, LAT:] = tail[r * each : (r + 1) * each]
    first = first_ref[0]
    key_lane = iota((1, local), 1)
    for r in range(requests):
        usable = jnp.zeros((1, local), jnp.int32)
        for p in range(pages):
            page = first + p
            listed = pages_ref[r, 0] == page
            for j in range(1, pages_ref.shape[1]):
                listed = jnp.logical_or(listed, pages_ref[r, j] == page)
            filled = jnp.where(listed, jnp.clip(len_ref[r] - page * BLK, 0, BLK), 0)
            inside = (key_lane >= p * BLK) & (key_lane < p * BLK + filled)
            usable = jnp.where(inside, 1, usable)
        keep = usable > 0
        lat = lat_ref[r].reshape(local, LAT)
        tails = jnp.concatenate(
            [unpaired(keyrope_ref[r, p]) for p in range(pages)], axis=0
        )
        tails = jnp.where(iota((local, 128), 1) < ROPE, tails, 0.0).astype(BF16)
        s = lax.dot_general(q_ref[r, :, :LAT], lat, NT, preferred_element_type=F32)
        s = s + lax.dot_general(q_ref[r, :, LAT:], tails, NT, preferred_element_type=F32)
        s = jnp.where(keep, s, LOW)
        peak = jnp.max(s, axis=1, keepdims=True)
        peak_hi = peak.astype(BF16).astype(F32)
        peak_lo = (peak - peak_hi).astype(BF16).astype(F32)
        w = jnp.where(keep, jnp.exp2((s - (peak_hi + peak_lo)) * SCALE2), 0.0)
        total = jnp.sum(w, axis=1, keepdims=True)
        total_hi = total.astype(BF16).astype(F32)
        total_lo = total - total_hi
        o = jnp.dot(w.astype(BF16), lat, preferred_element_type=F32).astype(BF16)
        stat_lane = iota((heads * each, 128), 1)
        stat = jnp.where(stat_lane < 2 * heads, peak_hi, total_hi)
        low = jnp.where(stat_lane < 2 * heads, peak_lo, total_lo)
        stat = jnp.where(stat_lane % (2 * heads) < heads, stat, low)
        for h in range(heads):
            mix_ref[h, r * each : (r + 1) * each, :] = o[h * each : (h + 1) * each]
        merged = jnp.zeros((each, 128), F32)
        for h in range(heads):
            here = iota((each, 128), 1) % heads == h
            merged = jnp.where(here, stat[h * each : (h + 1) * each], merged)
        stat_ref[r * each : (r + 1) * each, :] = merged
    for h in range(heads):
        out_ref[:, h * VDIM : (h + 1) * VDIM] = jnp.dot(
            mix_ref[h], wuv_ref[h], preferred_element_type=F32
        ).astype(BF16)
    out_ref[:, heads * VDIM :] = stat_ref[...].astype(BF16)


def decode(page_lists, lengths, first, nope, rope, w_uk, w_uv, latents, ropes):
    rows = nope.shape[0]
    heads = w_uk.shape[0]
    requests = latents.shape[0]
    each = rows // requests
    operands = (nope, rope, w_uk, w_uv, latents, ropes)
    out = jax.ShapeDtypeStruct((rows, heads * VDIM + 128), BF16)
    return pl.pallas_call(
        decode_kernel,
        out_shape=out,
        grid=(1,),
        in_specs=[SMALL] * 3 + [whole(operand) for operand in operands],
        out_specs=whole(out),
        scratch_shapes=[
            pltpu.VMEM((requests, heads * each, WIDE), BF16),
            pltpu.VMEM((heads, rows, LAT), BF16),
            pltpu.VMEM((rows, 128), F32),
        ],
        cost_estimate=pl.CostEstimate(
            flops=1000000000, bytes_accessed=7 * 1024 * 1024, transcendentals=300000
        ),
        compiler_params=PARAMS,
        name="decode",
    )(page_lists, lengths, first, *operands)


def combine_kernel(parts_ref, out_ref):
    sources, rows = parts_ref.shape[0], parts_ref.shape[1]
    width = out_ref.shape[1]
    heads = width // VDIM
    for row in range(rows):
        part = parts_ref[:, row, :].astype(F32)
        stat = part[:, width:]
        peak = stat[:, :heads] + stat[:, heads : 2 * heads]
        total = stat[:, 2 * heads : 3 * heads] + stat[:, 3 * heads : 4 * heads]
        top = jnp.max(peak, axis=0, keepdims=True)
        factor = jnp.exp2((peak - top) * SCALE2)
        factor = factor / jnp.sum(factor * total, axis=0, keepdims=True)
        for h in range(heads):
            value = part[:, h * VDIM : (h + 1) * VDIM] * factor[:, h : h + 1]
            out_ref[row : row + 1, h * VDIM : (h + 1) * VDIM] = jnp.sum(
                value, axis=0, keepdims=True
            ).astype(BF16)


def combine(parts, width):
    out = jax.ShapeDtypeStruct((parts.shape[1], width), BF16)
    return pl.pallas_call(
        combine_kernel,
        out_shape=out,
        grid=(1,),
        in_specs=[whole(parts)],
        out_specs=whole(out),
        compiler_params=PARAMS,
        name="combine",
    )(parts)


def shifted(block, axis, distance):
    count = lax.axis_size(axis)
    return lax.ppermute(block, axis, [(i, (i + distance) % count) for i in range(count)])


def turned(block, axis, distance):
    count = lax.axis_size(axis)
    route = [
        (g * count + i, g * count + (i + (distance, -distance)[g]) % count)
        for g in (0, 1)
        for i in range(count)
    ]
    return lax.ppermute(block, ("grp", axis), route)


CTX = ("y", "z")


def after(value, *earlier):
    return lax.optimization_barrier((value, *earlier))[0]


def body(
    q_nope,
    q_rope,
    prompt_latent,
    prompt_rope,
    prompt_lists,
    owner_map,
    w_uk,
    w_uv,
    dec_nope,
    dec_rope,
    store_latent,
    store_rope,
    lengths,
    page_lists,
):
    y, z, me = lax.axis_index("y"), lax.axis_index("z"), lax.axis_index("hd")
    ys, zs, count = lax.axis_size("y"), lax.axis_size("z"), lax.axis_size("hd")
    ctx, contexts = y * zs + z, ys * zs
    block_count = contexts * count
    query_blocks = count
    turn = 1 - 2 * lax.axis_index("grp")
    here = me.reshape(1)
    ring = jnp.stack([me, turn])

    chunk = slices(prompt_latent[0], prompt_rope[0], zs * count)
    chunk = lax.all_to_all(chunk, ("z", "hd"), split_axis=0, concat_axis=0, tiled=True)

    requests, per_device = store_latent.shape[1], store_latent.shape[2]
    parts = decode(
        page_lists[0],
        lengths[0],
        (ctx * per_device).reshape(1),
        dec_nope[0],
        dec_rope[0],
        w_uk,
        w_uv,
        store_latent[0],
        store_rope[0].reshape(requests, per_device, BLK // 2, 128),
    )
    rows_total, wide = parts.shape
    parts = parts.reshape(contexts, rows_total // contexts, wide)

    shares = split(here, q_nope[0], q_rope[0], count)
    hop = turned(shares[2], "hd", 1)
    queries = [shares[0], shifted(shares[1], "hd", 1), None, shifted(shares[3], "hd", 3)]
    chunk = after(chunk, parts, hop)
    queries[2] = turned(hop, "hd", 1)
    near, back = turned(chunk, "y", 1), turned(chunk, "y", -1)
    parts = lax.all_to_all(parts, CTX, split_axis=0, concat_axis=0, tiled=True)
    far = turned(after(near, back, queries[2], parts), "y", 1)

    order = (me - jnp.arange(query_blocks, dtype=jnp.int32)) % count
    q = absorb(order, queries, w_uk)

    first_block = ctx * query_blocks
    listed = lax.dynamic_slice_in_dim(prompt_lists[0], first_block, query_blocks, 0)
    slot_count = 2 * block_count // contexts
    mine = (owner_map[0, :, 0] == ctx).astype(jnp.int32)
    ranking = jnp.cumsum(mine) - 1
    hit = (mine[None, :] == 1) & (
        ranking[None, :] == jnp.arange(slot_count, dtype=jnp.int32)[:, None]
    )
    pages = jnp.max(
        jnp.where(hit, jnp.arange(block_count, dtype=jnp.int32)[None, :], -1), axis=1
    )
    carrier = 2
    layout = [(TOPK,)] * query_blocks
    layout[carrier] = (TOPK, slot_count)
    wanted = jnp.concatenate(
        [listed[: carrier + 1].reshape(-1), pages, listed[carrier + 1 :].reshape(-1)]
    )
    row = zs * count
    codes = turn * (y - wanted // row) % ys * row + wanted % row
    codes = jnp.where(wanted < 0, -1, codes)

    codes = after(codes, q)
    dec_out = combine(parts, w_uv.shape[0] * VDIM)
    sets = select(codes, (chunk, near, far, back), tuple(layout))

    rings, mixtures = [], []

    def mix(index, *ready):
        ids = after(listed[index], *ready)
        at = (first_block + index).reshape(1)
        mixtures.append(attend(index, rings[index], ids, at, ring, q))

    def neighbours(block):
        return turned(block, "hd", 1), turned(block, "hd", -1)

    def close(index, *earlier):
        ahead, behind = near_sets[index]
        far = turned(after(ahead, behind, *earlier), "hd", 1)
        rings.append((sets[index], ahead, far, behind))

    near_sets = [neighbours(sets[0]), neighbours(sets[1])]
    close(0)
    close(1)
    near_sets.append(neighbours(after(sets[2], *near_sets[1])))
    near_sets.append(neighbours(after(sets[3], *near_sets[1], rings[0][2])))
    mix(0, *near_sets[1], dec_out)
    close(2, mixtures[0])
    mix(1)
    close(3, mixtures[1])
    mix(2, mixtures[1], *near_sets[3])
    landed = land(after(ring, mixtures[-1], rings[-1][2]), rings[carrier], slot_count)
    landed_latent, landed_rope = (lax.ppermute(x, "grp", [(0, 1), (1, 0)]) for x in landed)
    last = query_blocks - 1
    at = (first_block + last).reshape(1)
    pre_out = attend(last, rings[last], listed[last], at, ring, q, mixtures, w_uv)
    return (pre_out[None], dec_out[None], landed_latent[None], landed_rope[None])


def solution(mesh):
    mesh = Mesh(mesh.devices.reshape(2, 4, 8, 4), ("grp", *CTX, "hd"))
    in_specs = (
        P("grp", (*CTX, "hd"), None),
        P("grp", (*CTX, "hd"), None),
        P("grp", (*CTX, "hd"), None),
        P("grp", (*CTX, "hd"), None),
        P("grp", None, None),
        P("grp", None, None),
        P("hd", None, None),
        P("hd", None, None),
        P("grp", None, "hd"),
        P("grp", None, "hd"),
        P("grp", None, CTX, None, None),
        P("grp", None, CTX, None),
        P("grp", None),
        P("grp", None, None),
    )
    out_specs = (
        P("grp", CTX, "hd"),
        P("grp", CTX, "hd"),
        P("grp", CTX, None, None),
        P("grp", CTX, None),
    )
    return jax.shard_map(body, mesh=mesh, in_specs=in_specs, out_specs=out_specs, check_vma=False)
```

```python
import functools

import jax
import jax.numpy as jnp
from jax import lax
from jax.experimental import pallas as pl
from jax.experimental.pallas import tpu as pltpu
from jax.sharding import Mesh, PartitionSpec as P

NOPE = 128
ROPE = 64
LAT = 512
VDIM = 128
BLK = 64
TOPK = 16
WIDE = LAT + 128
KEYS = TOPK * BLK
FEAT = 128
RROWS = BLK // 8
PART = BLK + RROWS
SET = TOPK * PART
LOW = -1e30
SCALE = (NOPE + ROPE) ** (-0.5)
SCALE2 = SCALE * 1.4426950408889634
F32 = jnp.float32
BF16 = jnp.bfloat16
NT = (((1,), (1,)), ((), ()))


PARAMS = pltpu.CompilerParams(vmem_limit_bytes=60 * 1024 * 1024)


def iota(shape, dim):
    return lax.broadcasted_iota(jnp.int32, shape, dim)


def whole(array):
    return pl.BlockSpec(array.shape, lambda *_: (0,) * len(array.shape))


SMALL = pl.BlockSpec(memory_space=pltpu.SMEM)


def unpaired(pairs):
    row, column = iota((BLK, BLK // 2), 0), iota((BLK, BLK // 2), 1)
    spread = jnp.where(row // 2 == column, 1.0, 0.0).astype(BF16)
    twice = jnp.dot(spread, pairs, preferred_element_type=F32)
    odd = iota((BLK, 128), 0) % 2 == 1
    return jnp.where(odd, pltpu.roll(twice, ROPE, 1), twice)


def slice_kernel(lat_ref, rope_ref, out_ref):
    count = lat_ref.shape[1] // FEAT
    tokens = unpaired(rope_ref[...])
    lane = iota((RROWS, 128), 1)
    for q in range(count):
        low = tokens[2 * q * RROWS : (2 * q + 1) * RROWS]
        high = tokens[(2 * q + 1) * RROWS : (2 * q + 2) * RROWS]
        rope = jnp.where(lane < ROPE, low, pltpu.roll(high, ROPE, 1)).astype(BF16)
        for z in range(out_ref.shape[0] // count):
            out_ref[z * count + q, :BLK] = lat_ref[:, q * FEAT : (q + 1) * FEAT]
            out_ref[z * count + q, BLK:] = rope


def slices(latent, rope, copies):
    out = jax.ShapeDtypeStruct((copies, PART, FEAT), BF16)
    return pl.pallas_call(
        slice_kernel,
        out_shape=out,
        grid=(1,),
        in_specs=[whole(latent), whole(rope)],
        out_specs=whole(out),
        compiler_params=PARAMS,
        name="slices",
    )(latent, rope)


def select_kernel(layout, code_ref, own_ref, near_ref, far_ref, back_ref, *refs):
    out_refs, all_ref = refs[:-1], refs[-1]
    start = 0
    for ref in (own_ref, near_ref, far_ref, back_ref):
        all_ref[start : start + ref.shape[0]] = ref[...]
        start += ref.shape[0]
    place = 0
    for sets, out_ref in zip(layout, out_refs):
        first = 0
        for blocks in sets:
            for j in range(0, blocks, 2):
                tails = []
                for i in (j, j + 1):
                    code = code_ref[place]
                    place += 1
                    source = jnp.maximum(code, 0)
                    lat = all_ref[source, :BLK]
                    tail = all_ref[source, BLK:].astype(F32)
                    if blocks < TOPK:
                        lat = jnp.where(code >= 0, lat, jnp.zeros_like(lat))
                        tail = jnp.where(code >= 0, tail, jnp.zeros_like(tail))
                    out_ref[first + i * BLK : first + (i + 1) * BLK] = lat
                    tails.append(tail)
                base = first + blocks * BLK + j * RROWS
                out_ref[base : base + 2 * RROWS] = jnp.concatenate(tails, axis=0).astype(BF16)
            first += blocks * PART


def select(codes, gathered, layout):
    sources = sum(part.shape[0] for part in gathered)
    outs = [jax.ShapeDtypeStruct((sum(sets) * PART, FEAT), BF16) for sets in layout]
    return pl.pallas_call(
        functools.partial(select_kernel, layout),
        out_shape=outs,
        grid=(1,),
        in_specs=[SMALL] + [whole(part) for part in gathered],
        out_specs=[whole(out) for out in outs],
        scratch_shapes=[pltpu.VMEM((sources, PART, FEAT), BF16)],
        compiler_params=pltpu.CompilerParams(vmem_limit_bytes=16 * 1024 * 1024),
        name="select",
    )(codes, *gathered)


def quarter_of(me_ref, s):
    return lax.rem(me_ref[0] + 4 - me_ref[1] * s, 4)


def place_ropes(ref, quarter, rows):
    flat = rows.reshape(-1, 128)
    ref[:, 2 * quarter] = rows
    ref[:, 2 * quarter + 1] = pltpu.roll(flat, ROPE, 1).reshape(rows.shape)


def land_kernel(me_ref, *refs):
    parts = refs[:4]
    lat_ref, rope_ref, token_ref = refs[4:]
    slots = lat_ref.shape[0]
    for s, ref in enumerate(parts):
        q = quarter_of(me_ref, s)
        lat_ref[:, :, pl.ds(pl.multiple_of(q * FEAT, FEAT), FEAT)] = ref[: slots * BLK].reshape(
            slots, BLK, FEAT
        )
        place_ropes(token_ref, q, ref[slots * BLK :].astype(F32).reshape(slots, RROWS, 128))
    lane = iota((slots, 128), 1)
    for r in range(BLK // 2):
        octet, row = 2 * r // 8, 2 * r % 8
        even, odd = token_ref[:, octet, row, :], token_ref[:, octet, row + 1, :]
        both = jnp.where(lane < ROPE, even, pltpu.roll(odd, ROPE, 1))
        rope_ref[:, r * 128 : (r + 1) * 128] = both.astype(BF16)


def land(me, parts, slots):
    rows = slots * PART
    outs = (
        jax.ShapeDtypeStruct((slots, BLK, LAT), BF16),
        jax.ShapeDtypeStruct((slots, BLK * ROPE), BF16),
    )
    return pl.pallas_call(
        land_kernel,
        out_shape=outs,
        grid=(1,),
        in_specs=[SMALL] + [pl.BlockSpec((rows, FEAT), lambda c: (SET // rows, 0))] * len(parts),
        out_specs=tuple(whole(out) for out in outs),
        scratch_shapes=[pltpu.VMEM((slots, 8, 8, 128), F32)],
        compiler_params=PARAMS,
        name="land",
    )(me, *parts)


def split_kernel(me_ref, nope_ref, rope_ref, *out_refs):
    count = len(out_refs)
    nope, rope = nope_ref.shape[1] // count, rope_ref.shape[1] // count
    for s, out_ref in enumerate(out_refs):
        to = lax.rem(me_ref[0] + s, count)
        out_ref[:, :nope] = nope_ref[:, pl.ds(pl.multiple_of(to * nope, 128), nope)]
        out_ref[:, nope:] = rope_ref[:, pl.ds(pl.multiple_of(to * rope, 128), rope)]


def split(me, nope, rope, count):
    out = jax.ShapeDtypeStruct((nope.shape[0], (nope.shape[1] + rope.shape[1]) // count), BF16)
    return pl.pallas_call(
        split_kernel,
        out_shape=[out] * count,
        grid=(1,),
        in_specs=[SMALL, whole(nope), whole(rope)],
        out_specs=[whole(out)] * count,
        cost_estimate=pl.CostEstimate(
            flops=0, bytes_accessed=4 * (nope.size + rope.size), transcendentals=0
        ),
        compiler_params=PARAMS,
        name="split",
    )(me, nope, rope)


def absorb_kernel(order_ref, *refs):
    wuk_ref, out_ref = refs[-2:]
    blocks = out_ref.shape[0]
    nope = jnp.concatenate([ref[...] for ref in refs[:blocks]], axis=0)
    rope = jnp.concatenate([ref[...] for ref in refs[blocks : 2 * blocks]], axis=0).astype(F32)
    lane = iota((blocks * BLK, 128), 1)
    spot = iota((blocks * BLK, 128), 0) % BLK
    onehot = jnp.where(lane == spot + ROPE, 1.0, 0.0)
    for i in range(wuk_ref.shape[0]):
        part = rope[:, i // 2 * 128 : i // 2 * 128 + 128]
        if i % 2 == 1:
            part = pltpu.roll(part, ROPE, 1)
        tail = jnp.where(lane < ROPE, part, onehot).astype(BF16)
        absorbed = jnp.dot(
            nope[:, i * NOPE : (i + 1) * NOPE], wuk_ref[i], preferred_element_type=F32
        ).astype(BF16)
        rows = slice(i * BLK, (i + 1) * BLK)
        for b in range(blocks):
            out_ref[order_ref[b], rows, :LAT] = absorbed[b * BLK : (b + 1) * BLK]
            out_ref[order_ref[b], rows, LAT:] = tail[b * BLK : (b + 1) * BLK]


def absorb(order, queries, w_uk):
    blocks = len(queries)
    heads = w_uk.shape[0]
    some = 4
    rows = blocks * BLK * heads
    nope_spec = pl.BlockSpec((BLK, some * NOPE), lambda p: (0, p))
    rope_spec = pl.BlockSpec((BLK, some * ROPE), lambda p: (0, p + heads * NOPE // (some * ROPE)))
    return pl.pallas_call(
        absorb_kernel,
        out_shape=jax.ShapeDtypeStruct((blocks, heads * BLK, WIDE), BF16),
        grid=(heads // some,),
        in_specs=[SMALL]
        + [nope_spec] * blocks
        + [rope_spec] * blocks
        + [pl.BlockSpec((some, NOPE, LAT), lambda p: (p, 0, 0))],
        out_specs=pl.BlockSpec((blocks, some * BLK, WIDE), lambda p: (0, p, 0)),
        cost_estimate=pl.CostEstimate(
            flops=2 * rows * NOPE * LAT,
            bytes_accessed=rows * (WIDE + 192) * 2 + heads * NOPE * LAT * 2,
            transcendentals=0,
        ),
        compiler_params=pltpu.CompilerParams(vmem_limit_bytes=24 * 1024 * 1024),
        name="absorb",
    )(order, *queries, *queries, w_uk)


def attend_kernel(mixed, ids_ref, block_ref, me_ref, *refs):
    set_refs, q_ref, refs = refs[:4], refs[4], refs[4:]
    mix_refs, wuv_ref = refs[1 : 1 + mixed], refs[-4]
    out_ref, keys_ref, token_ref = refs[-3:]

    @pl.when(pl.program_id(0) == 0)
    def _():
        for s, ref in enumerate(set_refs):
            quarter = quarter_of(me_ref, s)
            keys_ref[:, pl.ds(pl.multiple_of(quarter * FEAT, FEAT), FEAT)] = ref[:KEYS]
            place_ropes(token_ref, quarter, ref[KEYS:].astype(F32).reshape(TOPK, RROWS, 128))
        lane = iota((BLK, 128), 1)
        row = iota((BLK, 128), 0)
        place = block_ref[0] * BLK
        for j in range(TOPK):
            late = row + ids_ref[j] * BLK > place + lane - ROPE
            bias = jnp.where(late, LOW, 0.0)
            tail = jnp.where(lane < ROPE, token_ref[j].reshape(BLK, 128), bias)
            keys_ref[j * BLK : (j + 1) * BLK, LAT:] = tail.astype(BF16)

    rows = 4 * BLK
    chunks = [slice(at, at + rows) for at in range(0, q_ref.shape[1], rows)]
    scores = [
        lax.dot_general(q_ref[0, chunk, :], keys_ref[...], NT, preferred_element_type=F32)
        for chunk in chunks
    ]
    for chunk, s in zip(chunks, scores):
        peak = jnp.max(s, axis=1, keepdims=True)
        w = jnp.exp2((s - peak) * SCALE2)
        total = jnp.sum(w, axis=1, keepdims=True)
        o = jnp.dot(w.astype(BF16), keys_ref[:, :LAT], preferred_element_type=F32)
        o = (o * (1.0 / total)).astype(BF16)
        if mixed == 0:
            out_ref[chunk] = o
            continue
        for i in range(rows // BLK):
            h = chunk.start // BLK + i
            here = slice(h * BLK, (h + 1) * BLK)
            mixture = jnp.concatenate(
                [ref[here] for ref in mix_refs] + [o[i * BLK : (i + 1) * BLK]], axis=0
            )
            out_ref[:, h * VDIM : (h + 1) * VDIM] = jnp.dot(
                mixture, wuv_ref[h], preferred_element_type=F32
            ).astype(BF16)


def attend(index, sets, ids, block, me, q, mixtures=(), w_uv=None):
    rows = q.shape[1]
    steps = 2
    some = rows // steps
    operands = [ids, block, me, *sets, q]
    in_specs = (
        [SMALL] * 3
        + [pl.BlockSpec((SET, FEAT), lambda c: (0, 0))] * len(sets)
        + [pl.BlockSpec((1, some, WIDE), lambda c: (index, c, 0))]
    )
    if mixtures:
        tokens, heads = (len(mixtures) + 1) * BLK, w_uv.shape[0]
        operands += [*mixtures, w_uv]
        in_specs += [pl.BlockSpec((some, LAT), lambda c: (c, 0))] * len(mixtures)
        in_specs.append(pl.BlockSpec((heads // steps, LAT, VDIM), lambda c: (c, 0, 0)))
        out_shape = jax.ShapeDtypeStruct((tokens, heads * VDIM), BF16)
        out_spec = pl.BlockSpec((tokens, heads // steps * VDIM), lambda c: (0, c))
    else:
        out_shape = jax.ShapeDtypeStruct((rows, LAT), BF16)
        out_spec = pl.BlockSpec((some, LAT), lambda c: (c, 0))
    return pl.pallas_call(
        functools.partial(attend_kernel, len(mixtures)),
        out_shape=out_shape,
        grid=(steps,),
        in_specs=in_specs,
        out_specs=out_spec,
        scratch_shapes=[pltpu.VMEM((KEYS, WIDE), BF16), pltpu.VMEM((TOPK, 8, 8, 128), F32)],
        cost_estimate=pl.CostEstimate(
            flops=2 * rows * KEYS * (WIDE + LAT),
            bytes_accessed=rows * (WIDE + LAT) * 2 + 4 * SET * FEAT * 2,
            transcendentals=rows * KEYS,
        ),
        compiler_params=PARAMS,
        name="attend",
    )(*operands)


def decode_kernel(pages_ref, len_ref, first_ref, nope_ref, rope_ref, wuk_ref, wuv_ref,
                  lat_ref, keyrope_ref, out_ref, q_ref, mix_ref, stat_ref):
    heads = wuk_ref.shape[0]
    rows_total = nope_ref.shape[0]
    requests, pages = lat_ref.shape[0], lat_ref.shape[1]
    each = rows_total // requests
    local = pages * BLK
    lane = iota((rows_total, 128), 1)
    for h in range(heads):
        pair = rope_ref[:, h // 2 * 128 : h // 2 * 128 + 128].astype(F32)
        if h % 2 == 1:
            pair = pltpu.roll(pair, ROPE, 1)
        absorbed = jnp.dot(
            nope_ref[:, h * NOPE : (h + 1) * NOPE], wuk_ref[h], preferred_element_type=F32
        ).astype(BF16)
        tail = jnp.where(lane < ROPE, pair, 0.0).astype(BF16)
        for r in range(requests):
            q_ref[r, h * each : (h + 1) * each, :LAT] = absorbed[r * each : (r + 1) * each]
            q_ref[r, h * each : (h + 1) * each, LAT:] = tail[r * each : (r + 1) * each]
    first = first_ref[0]
    key_lane = iota((1, local), 1)
    for r in range(requests):
        usable = jnp.zeros((1, local), jnp.int32)
        for p in range(pages):
            page = first + p
            listed = pages_ref[r, 0] == page
            for j in range(1, pages_ref.shape[1]):
                listed = jnp.logical_or(listed, pages_ref[r, j] == page)
            filled = jnp.where(listed, jnp.clip(len_ref[r] - page * BLK, 0, BLK), 0)
            inside = (key_lane >= p * BLK) & (key_lane < p * BLK + filled)
            usable = jnp.where(inside, 1, usable)
        keep = usable > 0
        lat = lat_ref[r].reshape(local, LAT)
        tails = jnp.concatenate(
            [unpaired(keyrope_ref[r, p]) for p in range(pages)], axis=0
        )
        tails = jnp.where(iota((local, 128), 1) < ROPE, tails, 0.0).astype(BF16)
        s = lax.dot_general(q_ref[r, :, :LAT], lat, NT, preferred_element_type=F32)
        s = s + lax.dot_general(q_ref[r, :, LAT:], tails, NT, preferred_element_type=F32)
        s = jnp.where(keep, s, LOW)
        peak = jnp.max(s, axis=1, keepdims=True)
        peak_hi = peak.astype(BF16).astype(F32)
        peak_lo = (peak - peak_hi).astype(BF16).astype(F32)
        w = jnp.where(keep, jnp.exp2((s - (peak_hi + peak_lo)) * SCALE2), 0.0)
        total = jnp.sum(w, axis=1, keepdims=True)
        total_hi = total.astype(BF16).astype(F32)
        total_lo = total - total_hi
        o = jnp.dot(w.astype(BF16), lat, preferred_element_type=F32).astype(BF16)
        stat_lane = iota((heads * each, 128), 1)
        stat = jnp.where(stat_lane < 2 * heads, peak_hi, total_hi)
        low = jnp.where(stat_lane < 2 * heads, peak_lo, total_lo)
        stat = jnp.where(stat_lane % (2 * heads) < heads, stat, low)
        for h in range(heads):
            mix_ref[h, r * each : (r + 1) * each, :] = o[h * each : (h + 1) * each]
        merged = jnp.zeros((each, 128), F32)
        for h in range(heads):
            here = iota((each, 128), 1) % heads == h
            merged = jnp.where(here, stat[h * each : (h + 1) * each], merged)
        stat_ref[r * each : (r + 1) * each, :] = merged
    for h in range(heads):
        out_ref[:, h * VDIM : (h + 1) * VDIM] = jnp.dot(
            mix_ref[h], wuv_ref[h], preferred_element_type=F32
        ).astype(BF16)
    out_ref[:, heads * VDIM :] = stat_ref[...].astype(BF16)


def decode(page_lists, lengths, first, nope, rope, w_uk, w_uv, latents, ropes):
    rows = nope.shape[0]
    heads = w_uk.shape[0]
    requests = latents.shape[0]
    each = rows // requests
    operands = (nope, rope, w_uk, w_uv, latents, ropes)
    out = jax.ShapeDtypeStruct((rows, heads * VDIM + 128), BF16)
    return pl.pallas_call(
        decode_kernel,
        out_shape=out,
        grid=(1,),
        in_specs=[SMALL] * 3 + [whole(operand) for operand in operands],
        out_specs=whole(out),
        scratch_shapes=[
            pltpu.VMEM((requests, heads * each, WIDE), BF16),
            pltpu.VMEM((heads, rows, LAT), BF16),
            pltpu.VMEM((rows, 128), F32),
        ],
        cost_estimate=pl.CostEstimate(
            flops=1000000000, bytes_accessed=7 * 1024 * 1024, transcendentals=300000
        ),
        compiler_params=PARAMS,
        name="decode",
    )(page_lists, lengths, first, *operands)


def combine_kernel(parts_ref, out_ref):
    sources, rows = parts_ref.shape[0], parts_ref.shape[1]
    width = out_ref.shape[1]
    heads = width // VDIM
    for row in range(rows):
        part = parts_ref[:, row, :].astype(F32)
        stat = part[:, width:]
        peak = stat[:, :heads] + stat[:, heads : 2 * heads]
        total = stat[:, 2 * heads : 3 * heads] + stat[:, 3 * heads : 4 * heads]
        top = jnp.max(peak, axis=0, keepdims=True)
        factor = jnp.exp2((peak - top) * SCALE2)
        factor = factor / jnp.sum(factor * total, axis=0, keepdims=True)
        for h in range(heads):
            value = part[:, h * VDIM : (h + 1) * VDIM] * factor[:, h : h + 1]
            out_ref[row : row + 1, h * VDIM : (h + 1) * VDIM] = jnp.sum(
                value, axis=0, keepdims=True
            ).astype(BF16)


def combine(parts, width):
    out = jax.ShapeDtypeStruct((parts.shape[1], width), BF16)
    return pl.pallas_call(
        combine_kernel,
        out_shape=out,
        grid=(1,),
        in_specs=[whole(parts)],
        out_specs=whole(out),
        compiler_params=PARAMS,
        name="combine",
    )(parts)


def shifted(block, axis, distance):
    count = lax.axis_size(axis)
    return lax.ppermute(block, axis, [(i, (i + distance) % count) for i in range(count)])


def turned(block, axis, distance):
    count = lax.axis_size(axis)
    route = [
        (g * count + i, g * count + (i + (distance, -distance)[g]) % count)
        for g in (0, 1)
        for i in range(count)
    ]
    return lax.ppermute(block, ("grp", axis), route)


CTX = ("y", "z")


def after(value, *earlier):
    return lax.optimization_barrier((value, *earlier))[0]


def body(
    q_nope,
    q_rope,
    prompt_latent,
    prompt_rope,
    prompt_lists,
    owner_map,
    w_uk,
    w_uv,
    dec_nope,
    dec_rope,
    store_latent,
    store_rope,
    lengths,
    page_lists,
):
    y, z, me = lax.axis_index("y"), lax.axis_index("z"), lax.axis_index("hd")
    ys, zs, count = lax.axis_size("y"), lax.axis_size("z"), lax.axis_size("hd")
    ctx, contexts = y * zs + z, ys * zs
    block_count = contexts * count
    query_blocks = count
    turn = 1 - 2 * lax.axis_index("grp")
    here = me.reshape(1)
    ring = jnp.stack([me, turn])

    chunk = slices(prompt_latent[0], prompt_rope[0], zs * count)
    chunk = lax.all_to_all(chunk, ("z", "hd"), split_axis=0, concat_axis=0, tiled=True)

    requests, per_device = store_latent.shape[1], store_latent.shape[2]
    parts = decode(
        page_lists[0],
        lengths[0],
        (ctx * per_device).reshape(1),
        dec_nope[0],
        dec_rope[0],
        w_uk,
        w_uv,
        store_latent[0],
        store_rope[0].reshape(requests, per_device, BLK // 2, 128),
    )
    rows_total, wide = parts.shape
    parts = parts.reshape(contexts, rows_total // contexts, wide)

    shares = split(here, q_nope[0], q_rope[0], count)
    hop = turned(shares[2], "hd", 1)
    queries = [shares[0], shifted(shares[1], "hd", 1), None, shifted(shares[3], "hd", 3)]
    chunk = after(chunk, parts, hop)
    queries[2] = turned(hop, "hd", 1)
    near, back = turned(chunk, "y", 1), turned(chunk, "y", -1)
    parts = lax.all_to_all(parts, CTX, split_axis=0, concat_axis=0, tiled=True)
    far = turned(after(near, back, queries[2], parts), "y", 1)

    order = (me - jnp.arange(query_blocks, dtype=jnp.int32)) % count
    q = absorb(order, queries, w_uk)

    first_block = ctx * query_blocks
    listed = lax.dynamic_slice_in_dim(prompt_lists[0], first_block, query_blocks, 0)
    slot_count = 2 * block_count // contexts
    mine = (owner_map[0, :, 0] == ctx).astype(jnp.int32)
    ranking = jnp.cumsum(mine) - 1
    hit = (mine[None, :] == 1) & (
        ranking[None, :] == jnp.arange(slot_count, dtype=jnp.int32)[:, None]
    )
    pages = jnp.max(
        jnp.where(hit, jnp.arange(block_count, dtype=jnp.int32)[None, :], -1), axis=1
    )
    carrier = 2
    layout = [(TOPK,)] * query_blocks
    layout[carrier] = (TOPK, slot_count)
    wanted = jnp.concatenate(
        [listed[: carrier + 1].reshape(-1), pages, listed[carrier + 1 :].reshape(-1)]
    )
    row = zs * count
    codes = turn * (y - wanted // row) % ys * row + wanted % row
    codes = jnp.where(wanted < 0, -1, codes)

    codes = after(codes, q)
    dec_out = combine(parts, w_uv.shape[0] * VDIM)
    sets = select(codes, (chunk, near, far, back), tuple(layout))

    rings, mixtures = [], []

    def mix(index, *ready):
        ids = after(listed[index], *ready)
        at = (first_block + index).reshape(1)
        mixtures.append(attend(index, rings[index], ids, at, ring, q))

    def neighbours(block):
        return turned(block, "hd", 1), turned(block, "hd", -1)

    def close(index, *earlier):
        ahead, behind = near_sets[index]
        far = turned(after(ahead, behind, *earlier), "hd", 1)
        rings.append((sets[index], ahead, far, behind))

    near_sets = [neighbours(sets[0]), neighbours(sets[1])]
    close(0, dec_out, ring)
    close(1)
    near_sets.append(neighbours(after(sets[2], *near_sets[1])))
    near_sets.append(neighbours(after(sets[3], *near_sets[1], rings[0][2])))
    mix(0, *near_sets[1])
    close(2, mixtures[0])
    mix(1)
    close(3, mixtures[1])
    mix(2, mixtures[1], *near_sets[3])
    landed = land(after(ring, mixtures[-1], rings[-1][2]), rings[carrier], slot_count)
    landed_latent, landed_rope = (lax.ppermute(x, "grp", [(0, 1), (1, 0)]) for x in landed)
    last = query_blocks - 1
    at = (first_block + last).reshape(1)
    pre_out = attend(last, rings[last], listed[last], at, ring, q, mixtures, w_uv)
    return (pre_out[None], dec_out[None], landed_latent[None], landed_rope[None])


def solution(mesh):
    mesh = Mesh(mesh.devices.reshape(2, 4, 8, 4), ("grp", *CTX, "hd"))
    in_specs = (
        P("grp", (*CTX, "hd"), None),
        P("grp", (*CTX, "hd"), None),
        P("grp", (*CTX, "hd"), None),
        P("grp", (*CTX, "hd"), None),
        P("grp", None, None),
        P("grp", None, None),
        P("hd", None, None),
        P("hd", None, None),
        P("grp", None, "hd"),
        P("grp", None, "hd"),
        P("grp", None, CTX, None, None),
        P("grp", None, CTX, None),
        P("grp", None),
        P("grp", None, None),
    )
    out_specs = (
        P("grp", CTX, "hd"),
        P("grp", CTX, "hd"),
        P("grp", CTX, None, None),
        P("grp", CTX, None),
    )
    return jax.shard_map(body, mesh=mesh, in_specs=in_specs, out_specs=out_specs, check_vma=False)
```
